32 devices in a mesh: lat: 8 (over z, y), tok: 4 (over x, core).
Axes of the slice: x: 2, y: 2, z: 4, core: 2. Of those that a mesh axis runs over, the one named last changes fastest.
Arguments:
- resid: bfloat16 [8192, 512], P('lat', 'tok'), may hold values from -6 to 6
- active_ids: int32 [512, 64], P('tok'), may hold values from 0 to 16383, all different within a row
- w_enc: bfloat16 [16384, 8192], P('lat', 'tok'), may hold values from -0.5 to 0.5
- w_dec: bfloat16 [16384, 8192], P('lat', 'tok'), may hold values from -0.0625 to 0.0625
- b_enc: float32 [16384], P('lat'), may hold values from -8 to 8
- b_dec: bfloat16 [8192], P('lat'), may hold values from -3 to 3
Outputs:
- grad_w_enc: bfloat16 [16384, 8192], P('lat', 'tok')
- grad_w_dec: bfloat16 [16384, 8192], P('lat', 'tok')
- grad_b_enc: float32 [16384], P('lat')
- grad_b_dec: float32 [8192], P('tok')
The draws below stay inside these ranges and needn't reach their ends.
Inputs may be any that keep to these rules, and one draw needn't show every extreme that they name: `active_ids`: the 64 latents of a token are distinct, and every latent is active for some token.
All inputs are finite; a program needn't handle non-finite values.
Results may differ from the reference program's by a relative error of at most 0.0068.
Values may be sent and summed in bfloat16 or wider, within the bound.
A program may use at most 256 MiB of HBM per device.

```python
import jax
import jax.numpy as jnp
from jax import lax

D = 8192
L = 16384
K = 64
TOKENS = 512


def levels(stream_key, shape, cuts, least, largest):
    def one(position, shards_of):
        heights = jax.random.uniform(jax.random.fold_in(jax.random.fold_in(stream_key, 6), position), (shards_of,), jnp.float32, least / len(cuts), largest / len(cuts))
        return jnp.repeat(jnp.exp(heights), shape[position] // shards_of).reshape((-1,) + (1,) * (len(shape) - position - 1))

    loudness = one(*cuts[0])
    for cut in cuts[1:]:
        loudness = loudness * one(*cut)
    return loudness


def picks_of(own_key, rows, count, top, lift):
    ranking = jax.random.permutation(jax.random.fold_in(own_key, 1), count)
    favour = ranking
    for power in range(3):
        favour = favour * favour // count
    favour = favour * lift // count
    lots = jax.random.randint(jax.random.fold_in(own_key, 2), (rows, count), 0, 4096) + favour
    holders = jax.random.permutation(jax.random.fold_in(own_key, 3), rows)[jnp.arange(count) % rows]
    lots = jnp.where(jnp.arange(rows)[:, None] == holders[None, :], 1 << 14, lots)
    merit = lots * count + jnp.arange(count)
    return lax.top_k(merit.astype(jnp.int32), top)[1].astype(jnp.int32)


def normal_values(own_key, dims, width, bound, cuts=(), kind=jnp.bfloat16):
    entries = jax.random.normal(own_key, dims, jnp.float32) * width
    if len(cuts) > 0:
        entries = levels(own_key, dims, cuts, -0.22, 0.18) * entries
    return jnp.clip(entries, min=-bound, max=bound).astype(kind)


def setup_inputs(seed: int = 0) -> dict:
    splits = jax.random.split(jax.random.key(seed), 7)
    return {
        "resid": normal_values(splits[0], (D, TOKENS), 1.0, 6.0, ((0, 8), (1, 4))),
        "active_ids": picks_of(splits[1], TOKENS, L, K, 64),
        "w_enc": normal_values(splits[2], (L, D), 128 ** -0.5, 0.5, ((0, 8), (1, 4))),
        "w_dec": normal_values(splits[3], (L, D), D ** -0.5, 0.0625, ((0, 8), (1, 4))),
        "b_enc": normal_values(splits[4], (L,), 2.0, 8.0, ((0, 8),), jnp.float32),
        "b_dec": normal_values(splits[5], (D,), 0.5, 3.0, ((0, 8),)),
    }


def reference(resid, active_ids, w_enc, w_dec, b_enc, b_dec):
    f32 = jnp.float32
    bf16 = jnp.bfloat16
    centred = (resid.astype(f32) - b_dec.astype(f32)[:, None]).astype(bf16)
    pre = jnp.dot(w_enc, centred, preferred_element_type=f32) + b_enc[:, None]
    columns = jnp.broadcast_to(jnp.arange(TOKENS, dtype=jnp.int32)[:, None], active_ids.shape)
    active = jnp.zeros((L, TOKENS), f32).at[active_ids, columns].add(1.0)
    codes = (pre * active).astype(bf16)
    recon = lax.dot_general(w_dec, codes, (((0,), (0,)), ((), ())), preferred_element_type=f32)
    errors = (recon + b_dec.astype(f32)[:, None] - resid.astype(f32)).astype(bf16)
    grad_code = jnp.dot(w_dec, errors, preferred_element_type=f32)
    grad_pre = (grad_code * active).astype(bf16)
    grad_w_dec = lax.dot_general(codes, errors, (((1,), (1,)), ((), ())), preferred_element_type=f32).astype(bf16)
    grad_w_enc = lax.dot_general(grad_pre, centred, (((1,), (1,)), ((), ())), preferred_element_type=f32).astype(bf16)
    grad_b_enc = jnp.sum(grad_pre.astype(f32), axis=1)
    back = jnp.dot(grad_b_enc, w_enc.astype(f32), precision=lax.Precision.HIGHEST)
    grad_b_dec = jnp.sum(errors.astype(f32), axis=1) - back
    return grad_w_enc, grad_w_dec, grad_b_enc, grad_b_dec
```

```python
import jax
import jax.numpy as jnp
from jax import lax
from jax.sharding import PartitionSpec as P

f32 = jnp.float32
bf16 = jnp.bfloat16


def active_rows(ids, base, rows):
    word = 32 if rows % 32 == 0 else rows
    local = ids - base
    which = local // word
    place = local - which * word
    bit = lax.shift_left(jnp.int32(1), place)
    words = lax.iota(jnp.int32, rows // word)
    held = jnp.where(which[None, :, :] == words[:, None, None], bit[None, :, :], 0)
    held = jnp.sum(held, axis=1)
    shifts = lax.iota(jnp.int32, word)
    flags = lax.shift_right_logical(held[:, None, :], jnp.broadcast_to(shifts[None, :, None], (rows // word, word, held.shape[1]))) & 1
    return flags.reshape(rows, held.shape[1]).astype(f32)


def on_device(resid, active_ids, w_enc, w_dec, b_enc, b_dec):
    block_rows = w_enc.shape[0]
    width = w_enc.shape[1]
    lat_pos = lax.axis_index("lat")
    tok_pos = lax.axis_index("tok")
    tok_count = lax.axis_size("tok")
    lat_count = lax.axis_size("lat")
    rows = block_rows // tok_count
    feats = width // lat_count

    ids_all = lax.all_gather(active_ids, "tok", axis=0, tiled=True).T
    bias_full = lax.all_gather(b_dec, "lat", axis=0, tiled=True)
    resid_full = lax.all_gather(resid, "lat", axis=0, tiled=True)
    resid_mine = lax.all_to_all(resid_full, "tok", split_axis=0, concat_axis=1, tiled=True)
    bias_mine = lax.dynamic_slice_in_dim(bias_full, tok_pos * width, width, 0)
    centred = (resid_mine.astype(f32) - bias_mine.astype(f32)[:, None]).astype(bf16)

    active = active_rows(ids_all, lat_pos * block_rows + tok_pos * rows, rows)
    b_rows = lax.dynamic_slice_in_dim(b_enc, tok_pos * rows, rows, 0)

    pre_part = jnp.dot(w_enc, centred, preferred_element_type=f32).astype(bf16)
    pre = lax.psum_scatter(pre_part, "tok", scatter_dimension=0, tiled=True)
    codes_rows = ((pre.astype(f32) + b_rows[:, None]) * active).astype(bf16)
    codes = lax.all_gather(codes_rows, "tok", axis=0, tiled=True)

    recon_part = lax.dot_general(
        w_dec, codes, (((0,), (0,)), ((), ())), preferred_element_type=f32
    ).astype(bf16)
    recon = lax.psum_scatter(recon_part, "lat", scatter_dimension=0, tiled=True)
    r_rows = lax.dynamic_slice_in_dim(resid_mine, lat_pos * feats, feats, 0)
    bd_rows = lax.dynamic_slice_in_dim(bias_mine, lat_pos * feats, feats, 0)
    error_rows = (
        recon.astype(f32) + bd_rows.astype(f32)[:, None] - r_rows.astype(f32)
    ).astype(bf16)
    errors = lax.all_gather(error_rows, "lat", axis=0, tiled=True)

    gc_part = jnp.dot(w_dec, errors, preferred_element_type=f32).astype(bf16)
    gc = lax.psum_scatter(gc_part, "tok", scatter_dimension=0, tiled=True)
    gp_rows = (gc.astype(f32) * active).astype(bf16)
    grad_pre = lax.all_gather(gp_rows, "tok", axis=0, tiled=True)

    grad_w_dec = lax.dot_general(
        codes, errors, (((1,), (1,)), ((), ())), preferred_element_type=f32
    ).astype(bf16)
    grad_b_enc = jnp.sum(grad_pre.astype(f32), axis=1)
    high = grad_b_enc.astype(bf16)
    rest = grad_b_enc - high.astype(f32)
    mid = rest.astype(bf16)
    low = (rest - mid.astype(f32)).astype(bf16)
    parts = jnp.stack([high, mid, low])
    back = jnp.sum(jnp.dot(parts, w_enc, preferred_element_type=f32), axis=0)
    back = lax.psum(back, "lat")
    error_total = jnp.sum(errors.astype(f32), axis=1)
    grad_w_enc = lax.dot_general(
        grad_pre, centred, (((1,), (1,)), ((), ())), preferred_element_type=f32
    ).astype(bf16)
    return (grad_w_enc, grad_w_dec, grad_b_enc, error_total - back)


def solution(mesh):
    return jax.shard_map(
        on_device,
        mesh=mesh,
        in_specs=(
            P("lat", "tok"),
            P("tok", None),
            P("lat", "tok"),
            P("lat", "tok"),
            P("lat"),
            P("lat"),
        ),
        out_specs=(P("lat", "tok"), P("lat", "tok"), P("lat"), P("tok")),
        check_vma=False,
    )
```

```python
import functools

import jax
import jax.numpy as jnp
from jax import lax
from jax.experimental import pallas as pl
from jax.experimental.pallas import tpu as pltpu
from jax.sharding import PartitionSpec as P

f32 = jnp.float32
bf16 = jnp.bfloat16
MESH = pl.DeviceIdType.MESH
DMA = pltpu.SemaphoreType.DMA
VMEM = pltpu.VMEM


def remote(src, dst, send, recv, lat, tok):
    return pltpu.make_async_remote_copy(
        src_ref=src, dst_ref=dst, send_sem=send, recv_sem=recv,
        device_id=(lat, tok), device_id_type=MESH,
    )


def greet(devices):
    barrier = pltpu.get_barrier_semaphore()
    for lat, tok in devices:
        pl.semaphore_signal(barrier, inc=1, device_id=(lat, tok), device_id_type=MESH)
    pl.semaphore_wait(barrier, len(devices))


def column(lat, tok, count):
    return [(lax.rem(lat + s, count), tok) for s in range(1, count)]


def group(lat, tok, count):
    return [(lat, lax.rem(tok + s, count)) for s in range(1, count)]


def call(kernel, out_shape, inputs, scratch, ident, name):
    return pl.pallas_call(
        kernel,
        out_shape=out_shape,
        in_specs=[pl.BlockSpec(memory_space=VMEM)] * len(inputs),
        out_specs=pl.BlockSpec(memory_space=VMEM),
        scratch_shapes=scratch,
        compiler_params=pltpu.CompilerParams(
            collective_id=ident, has_side_effects=True, vmem_limit_bytes=40 * 2**20
        ),
        name=name,
    )(*inputs)


def spread_kernel(x_ref, out_ref, own_sem, first_send, up_send, down_send, side_send, recv):
    lat, tok = lax.axis_index("lat"), lax.axis_index("tok")
    z, y = lat // 2, lat % 2
    rows, cols = x_ref.shape
    greet(column(lat, tok, 8) + group(lat, tok, 4))

    def place(half, part):
        return out_ref.at[
            pl.ds(pl.multiple_of(half * rows, rows), rows),
            pl.ds(pl.multiple_of(part * cols, cols), cols),
        ]

    home = remote(x_ref, place(y, tok), first_send, recv.at[y * 4 + tok], lat, z)
    own = pltpu.make_async_copy(x_ref, place(y, tok), own_sem)

    @pl.when(tok != z)
    def _():
        home.start()

    @pl.when(tok == z)
    def _():
        own.start()

    goes_up = jnp.logical_and(z >= tok, z < 3)
    goes_down = jnp.logical_and(z <= tok, z > 0)
    moves = []
    for k in range(4):
        part = lax.rem(tok + k, 4)
        here = place(y, part)
        arrived = recv.at[y * 4 + part]
        up = remote(here, here, up_send.at[k], arrived, lat + 2, tok)
        down = remote(here, here, down_send.at[k], arrived, lat - 2, tok)
        side = remote(here, here, side_send.at[k], arrived, lat + 1 - 2 * y, tok)
        if k == 0:
            @pl.when(tok == z)
            def _():
                own.wait()

            @pl.when(tok != z)
            def _():
                side.wait_recv()
        else:
            side.wait_recv()

        @pl.when(goes_up)
        def _():
            up.start()

        @pl.when(goes_down)
        def _():
            down.start()

        side.start()
        moves.append((up, down, side))
    for k in range(4):
        part = lax.rem(tok + k, 4)
        there = place(1 - y, part)
        remote(there, there, side_send.at[k], recv.at[(1 - y) * 4 + part], lat, tok).wait_recv()
    for up, down, side in moves:
        @pl.when(goes_up)
        def _():
            up.wait_send()

        @pl.when(goes_down)
        def _():
            down.wait_send()

        side.wait_send()

    @pl.when(tok != z)
    def _():
        home.wait_send()


def spread(resid):
    rows, cols = resid.shape
    return call(
        spread_kernel,
        jax.ShapeDtypeStruct((2 * rows, 4 * cols), resid.dtype),
        (resid,),
        [DMA, DMA, DMA((4,)), DMA((4,)), DMA((4,)), DMA((8,))],
        1,
        "spread_features",
    )


def masked_sum_kernel(
    part_ref, bias_ref, active_ref, out_ref,
    near, sent, far, near_send, near_recv, far_send, far_recv,
    x_send, x_recv, c_send, c_recv, f_send, f_recv,
):
    lat, tok = lax.axis_index("lat"), lax.axis_index("tok")
    x, c = tok // 2, tok % 2
    ox, oc = 1 - x, 1 - c
    pair, across = x * 2 + oc, ox * 2 + c
    rows = part_ref.shape[1]
    half = rows // 2
    greet([(lat, pair), (lat, across)])

    swaps = []
    for n, bx in ((0, ox), (1, x)):
        swap = remote(
            part_ref.at[bx * 2 + oc], near.at[n], near_send.at[n], near_recv.at[n], lat, pair
        )
        swap.start()
        swaps.append(swap)
    swaps[0].wait_recv()
    cuts = [pl.ds(n * half, half) for n in range(2)]
    outs = []
    for n, cut in enumerate(cuts):
        sent[cut, :] = (
            part_ref[across, cut, :].astype(f32) + near[0, cut, :].astype(f32)
        ).astype(bf16)
        move = remote(
            sent.at[cut], far.at[cut], far_send.at[n], far_recv.at[n], lat, across
        )
        move.start()
        outs.append(move)
    swaps[1].wait_recv()
    gives = []
    for n, cut in enumerate(cuts):
        outs[n].wait_recv()
        total = (
            part_ref[tok, cut, :].astype(f32)
            + near[1, cut, :].astype(f32)
            + far[cut, :].astype(f32)
        )
        out_ref[tok, cut, :] = ((total + bias_ref[cut, :]) * active_ref[cut, :]).astype(bf16)
        mine = out_ref.at[tok, cut]
        for give in (
            remote(mine, mine, x_send.at[n], x_recv.at[n], lat, across),
            remote(mine, mine, c_send.at[n], c_recv.at[n], lat, pair),
        ):
            give.start()
            gives.append(give)
    for n, cut in enumerate(cuts):
        got = out_ref.at[across, cut]
        remote(got, got, x_send.at[n], x_recv.at[n], lat, across).wait_recv()
        give = remote(got, got, f_send.at[n], f_recv.at[n], lat, pair)
        give.start()
        gives.append(give)
    for n, cut in enumerate(cuts):
        got = out_ref.at[pair, cut]
        remote(got, got, c_send.at[n], c_recv.at[n], lat, pair).wait_recv()
        got = out_ref.at[ox * 2 + oc, cut]
        remote(got, got, f_send.at[n], f_recv.at[n], lat, pair).wait_recv()
    for move in swaps + outs + gives:
        move.wait_send()


def masked_sum(part, bias, active, ident):
    total, tokens = part.shape
    rows = total // 4
    return call(
        masked_sum_kernel,
        jax.ShapeDtypeStruct((4, rows, tokens), bf16),
        (part.reshape(4, rows, tokens), bias, active),
        [VMEM((2, rows, tokens), bf16), VMEM((rows, tokens), bf16), VMEM((rows, tokens), bf16)]
        + [DMA((2,))] * 10,
        ident,
        "masked_sum_%d" % ident,
    ).reshape(total, tokens)


def errors_kernel(
    part_ref, bias_ref, resid_ref, out_ref,
    side, below, above, sent,
    side_send, side_recv, line_send, below_recv, above_recv,
    up_send, down_send, turn_send, gather_recv,
):
    lat, tok = lax.axis_index("lat"), lax.axis_index("tok")
    z, y = lat // 2, lat % 2
    oy = 1 - y
    beside = z * 2 + oy
    greet(column(lat, tok, 8))
    high = z // 2
    order = (3 - 3 * high, 2 - high, 1 - z + 4 * high, z)

    swaps = []
    for d in order:
        swap = remote(
            part_ref.at[d * 2 + oy], side.at[d], side_send.at[d], side_recv.at[d], beside, tok
        )
        swap.start()
        swaps.append(swap)

    def held(d):
        return part_ref[d * 2 + y].astype(f32) + side[d].astype(f32)

    lines = []
    for d, swap in zip(order[:3], swaps[:3]):
        swap.wait_recv()
        up = remote(sent.at[d], below.at[d], line_send.at[d], below_recv.at[d], lat + 2, tok)
        down = remote(sent.at[d], above.at[d], line_send.at[d], above_recv.at[d], lat - 2, tok)
        sent[d] = held(d).astype(bf16)

        @pl.when(jnp.logical_and(d > z, z > 0))
        def _():
            up.wait_recv()
            sent[d] = (held(d) + below[d].astype(f32)).astype(bf16)

        @pl.when(jnp.logical_and(d < z, z < 3))
        def _():
            down.wait_recv()
            sent[d] = (held(d) + above[d].astype(f32)).astype(bf16)

        @pl.when(d > z)
        def _():
            up.start()

        @pl.when(d < z)
        def _():
            down.start()

        lines.append((d, up, down))
    swaps[3].wait_recv()

    from_below = remote(sent.at[z], below.at[z], line_send.at[z], below_recv.at[z], lat, tok)
    from_above = remote(sent.at[z], above.at[z], line_send.at[z], above_recv.at[z], lat, tok)

    def finish(total):
        out_ref[lat] = (total + bias_ref[...] - resid_ref[...].astype(f32)).astype(bf16)

    @pl.when(z == 0)
    def _():
        from_above.wait_recv()
        finish(held(z) + above[z].astype(f32))

    @pl.when(z == 3)
    def _():
        from_below.wait_recv()
        finish(held(z) + below[z].astype(f32))

    @pl.when(jnp.logical_and(z > 0, z < 3))
    def _():
        from_below.wait_recv()
        from_above.wait_recv()
        finish(held(z) + below[z].astype(f32) + above[z].astype(f32))

    def relay(o):
        here = out_ref.at[o * 2 + y]
        arrived = gather_recv.at[o * 2 + y]
        return (
            remote(here, here, up_send.at[o], arrived, lat + 2, tok),
            remote(here, here, down_send.at[o], arrived, lat - 2, tok),
            remote(here, here, turn_send.at[o], arrived, beside, tok),
        )

    up, down, turn = relay(z)
    pl.when(z < 3)(up.start)
    pl.when(z > 0)(down.start)
    turn.start()
    for s in range(1, 4):
        @pl.when(z - s >= 0)
        def _():
            up, down, turn = relay(z - s)
            turn.wait_recv()
            pl.when(z < 3)(up.start)
            turn.start()

        @pl.when(z + s <= 3)
        def _():
            up, down, turn = relay(z + s)
            turn.wait_recv()
            pl.when(z > 0)(down.start)
            turn.start()

    for o in range(4):
        there = out_ref.at[o * 2 + oy]
        remote(there, there, turn_send.at[o], gather_recv.at[o * 2 + oy], beside, tok).wait_recv()
    for o in range(4):
        up, down, turn = relay(o)
        pl.when(jnp.logical_and(o <= z, z < 3))(up.wait_send)
        pl.when(jnp.logical_and(o >= z, z > 0))(down.wait_send)
        turn.wait_send()
    for swap in swaps:
        swap.wait_send()
    for d, up, down in lines:
        up.wait_send()


def errors_of(part, bias, resid_rows):
    total, tokens = part.shape
    rows = total // 8
    return call(
        errors_kernel,
        jax.ShapeDtypeStruct((8, rows, tokens), bf16),
        (part.reshape(8, rows, tokens), bias, resid_rows),
        [VMEM((4, rows, tokens), bf16)] * 4 + [DMA((4,))] * 8 + [DMA((8,))],
        4,
        "recon_errors",
    ).reshape(total, tokens)


def small_sum_kernel(x_ref, out_ref, held, send, recv):
    lat, tok = lax.axis_index("lat"), lax.axis_index("tok")
    greet(column(lat, tok, 8))
    moves = []
    for s in range(1, 8):
        move = remote(
            x_ref, held.at[s], send.at[s], recv.at[s], lax.rem(lat + s, 8), tok
        )
        move.start()
        moves.append(move)
    held[0] = x_ref[...]
    for move in moves:
        move.wait_recv()
    out_ref[...] = jnp.sum(held[...], axis=0)
    for move in moves:
        move.wait_send()


def small_sum(x):
    wide = x.reshape(x.shape[0] // 128, 128)
    return call(
        small_sum_kernel,
        jax.ShapeDtypeStruct(wide.shape, f32),
        (wide,),
        [VMEM((8,) + wide.shape, f32), DMA((8,)), DMA((8,))],
        5,
        "small_sum",
    ).reshape(x.shape)


def active_rows(ids, base, rows):
    word = 32 if rows % 32 == 0 else rows
    local = ids - base
    which = local // word
    place = local - which * word
    bit = lax.shift_left(jnp.int32(1), place)
    words = lax.iota(jnp.int32, rows // word)
    held = jnp.where(which[None, :, :] == words[:, None, None], bit[None, :, :], 0)
    held = jnp.sum(held, axis=1)
    shifts = lax.iota(jnp.int32, word)
    flags = lax.shift_right_logical(held[:, None, :], jnp.broadcast_to(shifts[None, :, None], (rows // word, word, held.shape[1]))) & 1
    return flags.reshape(rows, held.shape[1]).astype(f32)


def on_device(kernels, resid, active_ids, w_enc, w_dec, b_enc, b_dec):
    block_rows = w_enc.shape[0]
    width = w_enc.shape[1]
    lat_pos = lax.axis_index("lat")
    tok_pos = lax.axis_index("tok")
    tok_count = lax.axis_size("tok")
    lat_count = lax.axis_size("lat")
    rows = block_rows // tok_count
    feats = width // lat_count

    ids_all = lax.all_gather(active_ids, "tok", axis=0, tiled=True).T
    bias_full = lax.all_gather(b_dec, "lat", axis=0, tiled=True)
    if kernels:
        resid_mine = spread(resid)
    else:
        resid_full = lax.all_gather(resid, "lat", axis=0, tiled=True)
        resid_mine = lax.all_to_all(resid_full, "tok", split_axis=0, concat_axis=1, tiled=True)
    bias_mine = lax.dynamic_slice_in_dim(bias_full, tok_pos * width, width, 0)
    centred = (resid_mine.astype(f32) - bias_mine.astype(f32)[:, None]).astype(bf16)

    active = active_rows(ids_all, lat_pos * block_rows + tok_pos * rows, rows)
    b_rows = lax.dynamic_slice_in_dim(b_enc, tok_pos * rows, rows, 0)

    pre_part = jnp.dot(w_enc, centred, preferred_element_type=f32).astype(bf16)
    if kernels:
        codes = masked_sum(pre_part, b_rows[:, None], active, 2)
    else:
        pre = lax.psum_scatter(pre_part.astype(f32), "tok", scatter_dimension=0, tiled=True)
        codes_rows = ((pre + b_rows[:, None]) * active).astype(bf16)
        codes = lax.all_gather(codes_rows, "tok", axis=0, tiled=True)

    recon_part = lax.dot_general(
        w_dec, codes, (((0,), (0,)), ((), ())), preferred_element_type=f32
    ).astype(bf16)
    r_rows = lax.dynamic_slice_in_dim(resid_mine, lat_pos * feats, feats, 0)
    bd_rows = lax.dynamic_slice_in_dim(bias_mine, lat_pos * feats, feats, 0)
    bd_rows = bd_rows.astype(f32)[:, None]
    if kernels:
        errors = errors_of(recon_part, bd_rows, r_rows)
    else:
        recon = lax.psum_scatter(
            recon_part.astype(f32), "lat", scatter_dimension=0, tiled=True
        )
        error_rows = (recon + bd_rows - r_rows.astype(f32)).astype(bf16)
        errors = lax.all_gather(error_rows, "lat", axis=0, tiled=True)

    gc_part = jnp.dot(w_dec, errors, preferred_element_type=f32).astype(bf16)
    if kernels:
        grad_pre = masked_sum(gc_part, jnp.zeros((rows, 1), f32), active, 3)
    else:
        gc = lax.psum_scatter(gc_part.astype(f32), "tok", scatter_dimension=0, tiled=True)
        gp_rows = (gc * active).astype(bf16)
        grad_pre = lax.all_gather(gp_rows, "tok", axis=0, tiled=True)

    grad_w_dec = lax.dot_general(
        codes, errors, (((1,), (1,)), ((), ())), preferred_element_type=f32
    ).astype(bf16)
    grad_b_enc = jnp.sum(grad_pre.astype(f32), axis=1)
    high = grad_b_enc.astype(bf16)
    rest = grad_b_enc - high.astype(f32)
    mid = rest.astype(bf16)
    low = (rest - mid.astype(f32)).astype(bf16)
    parts = jnp.stack([high, mid, low])
    back = jnp.sum(jnp.dot(parts, w_enc, preferred_element_type=f32), axis=0)
    back = small_sum(back) if kernels else lax.psum(back, "lat")
    error_total = jnp.sum(errors.astype(f32), axis=1)
    grad_w_enc = lax.dot_general(
        grad_pre, centred, (((1,), (1,)), ((), ())), preferred_element_type=f32
    ).astype(bf16)
    return (grad_w_enc, grad_w_dec, grad_b_enc, error_total - back)


def solution(mesh):
    kernels = mesh.shape["lat"] == 8 and mesh.shape["tok"] == 4
    return jax.shard_map(
        functools.partial(on_device, kernels),
        mesh=mesh,
        in_specs=(
            P("lat", "tok"),
            P("tok", None),
            P("lat", "tok"),
            P("lat", "tok"),
            P("lat"),
            P("lat"),
        ),
        out_specs=(P("lat", "tok"), P("lat", "tok"), P("lat"), P("tok")),
        check_vma=False,
    )
```

```python
import functools

import jax
import jax.numpy as jnp
from jax import lax
from jax.experimental import pallas as pl
from jax.experimental.pallas import tpu as pltpu
from jax.sharding import PartitionSpec as P

f32 = jnp.float32
bf16 = jnp.bfloat16
MESH = pl.DeviceIdType.MESH
DMA = pltpu.SemaphoreType.DMA
VMEM = pltpu.VMEM


def remote(src, dst, send, recv, lat, tok):
    return pltpu.make_async_remote_copy(
        src_ref=src, dst_ref=dst, send_sem=send, recv_sem=recv,
        device_id=(lat, tok), device_id_type=MESH,
    )


def greet(devices):
    barrier = pltpu.get_barrier_semaphore()
    for lat, tok in devices:
        pl.semaphore_signal(barrier, inc=1, device_id=(lat, tok), device_id_type=MESH)
    pl.semaphore_wait(barrier, len(devices))


def column(lat, tok, count):
    return [(lax.rem(lat + s, count), tok) for s in range(1, count)]


def group(lat, tok, count):
    return [(lat, lax.rem(tok + s, count)) for s in range(1, count)]


def call(kernel, out_shape, inputs, scratch, ident, name, whole=()):
    return pl.pallas_call(
        kernel,
        out_shape=out_shape,
        in_specs=[
            pl.BlockSpec(memory_space=pl.ANY if n in whole else VMEM)
            for n in range(len(inputs))
        ],
        out_specs=jax.tree.map(lambda _: pl.BlockSpec(memory_space=VMEM), out_shape),
        scratch_shapes=scratch,
        compiler_params=pltpu.CompilerParams(
            collective_id=ident, has_side_effects=True, vmem_limit_bytes=44 * 2**20
        ),
        name=name,
    )(*inputs)


def spread_kernel(
    x_ref, bias_ref, ids_ref, out_ref, bias_out, ids_out,
    own_sem, first_send, up_send, down_send, side_send, recv,
    bias_send, bias_recv, ids_send, ids_recv,
):
    lat, tok = lax.axis_index("lat"), lax.axis_index("tok")
    z, y = lat // 2, lat % 2
    rows, cols = x_ref.shape
    pieces = 2
    cut = rows // pieces
    greet(column(lat, tok, 8) + group(lat, tok, 4))

    def place(half, part, n):
        return out_ref.at[
            pl.ds(pl.multiple_of(half * rows + n * cut, cut), cut),
            pl.ds(pl.multiple_of(part * cols, cols), cols),
        ]

    def sem_of(half, part, n):
        return recv.at[half * (4 * pieces) + part * pieces + n]

    firsts = []
    for n in range(pieces):
        mine = x_ref.at[pl.ds(n * cut, cut)]
        home = remote(mine, place(y, tok, n), first_send.at[n], sem_of(y, tok, n), lat, z)
        own = pltpu.make_async_copy(mine, place(y, tok, n), own_sem.at[n])
        pl.when(tok != z)(home.start)
        pl.when(tok == z)(own.start)
        firsts.append((home, own))

    bias_moves = [
        remote(bias_ref, bias_out.at[y], bias_send.at[s], bias_recv.at[y], lax.rem(lat + s, 8), tok)
        for s in range(1, 8)
    ]

    @pl.when(tok == z)
    def _():
        for move in bias_moves:
            move.start()
        bias_out[y] = bias_ref[...]

    def ids_place(part):
        return ids_out.at[:, pl.ds(pl.multiple_of(part * cols, cols), cols)]

    ids_moves = []
    for s in range(1, 4):
        move = remote(
            ids_ref, ids_place(tok), ids_send.at[s], ids_recv.at[s], lat, lax.rem(tok + s, 4)
        )
        move.start()
        ids_moves.append(move)
    ids_out[:, pl.ds(pl.multiple_of(tok * cols, cols), cols)] = ids_ref[...]

    goes_up = jnp.logical_and(z >= tok, z < 3)
    goes_down = jnp.logical_and(z <= tok, z > 0)
    moves = []
    for k in range(4):
        part = lax.rem(tok + k, 4)
        for n in range(pieces):
            m = k * pieces + n
            here = place(y, part, n)
            arrived = sem_of(y, part, n)
            up = remote(here, here, up_send.at[m], arrived, lat + 2, tok)
            down = remote(here, here, down_send.at[m], arrived, lat - 2, tok)
            side = remote(here, here, side_send.at[m], arrived, lat + 1 - 2 * y, tok)
            if k == 0:
                pl.when(tok == z)(firsts[n][1].wait)
                pl.when(tok != z)(side.wait_recv)
            else:
                side.wait_recv()
            pl.when(goes_up)(up.start)
            pl.when(goes_down)(down.start)
            side.start()
            moves.append((up, down, side))
    for k in range(4):
        part = lax.rem(tok + k, 4)
        for n in range(pieces):
            there = place(1 - y, part, n)
            remote(
                there, there, side_send.at[0], sem_of(1 - y, part, n), lat, tok
            ).wait_recv()
    for h in range(2):
        @pl.when(jnp.logical_or(tok != z, y != h))
        def _():
            remote(
                bias_ref, bias_out.at[h], bias_send.at[0], bias_recv.at[h], lat, tok
            ).wait_recv()
    for move in ids_moves:
        move.wait_recv()
        move.wait_send()
    for up, down, side in moves:
        pl.when(goes_up)(up.wait_send)
        pl.when(goes_down)(down.wait_send)
        side.wait_send()
    for home, own in firsts:
        pl.when(tok != z)(home.wait_send)

    @pl.when(tok == z)
    def _():
        for move in bias_moves:
            move.wait_send()


def spread(resid, bias, ids):
    rows, cols = resid.shape
    wide = bias.astype(f32).reshape(rows // 128, 128)
    resid_mine, bias_mine, ids_all = call(
        spread_kernel,
        (
            jax.ShapeDtypeStruct((2 * rows, 4 * cols), resid.dtype),
            jax.ShapeDtypeStruct((2,) + wide.shape, f32),
            jax.ShapeDtypeStruct((ids.shape[1], 4 * cols), ids.dtype),
        ),
        (resid, wide, ids.T),
        [DMA((2,)), DMA((2,)), DMA((8,)), DMA((8,)), DMA((8,)), DMA((16,))]
        + [DMA((8,)), DMA((2,)), DMA((4,)), DMA((4,))],
        1,
        "spread_features",
    )
    return resid_mine, bias_mine.reshape(2 * rows), ids_all


def masked_sum_kernel(
    w_ref, act_ref, bias_ref, active_ref, out_ref,
    w, part_ref, w_sem, near, sent, far, near_send, near_recv, far_send, far_recv,
    x_send, x_recv, c_send, c_recv, f_send, f_recv,
):
    lat, tok = lax.axis_index("lat"), lax.axis_index("tok")
    x, c = tok // 2, tok % 2
    ox, oc = 1 - x, 1 - c
    pair, across = x * 2 + oc, ox * 2 + c
    rows = part_ref.shape[1]
    half = rows // 2
    order = (ox * 2 + oc, pair, across, tok)
    loads = []
    for n, block in enumerate(order):
        load = pltpu.make_async_copy(w_ref.at[block], w.at[n], w_sem.at[n])
        load.start()
        loads.append(load)
    greet([(lat, pair), (lat, across)])

    def multiply(n):
        loads[n].wait()

        def step(m, carry):
            cols = pl.ds(pl.multiple_of(m * 256, 256), 256)
            part_ref[order[n], :, cols] = jnp.dot(
                w[n], act_ref[:, cols], preferred_element_type=f32
            ).astype(bf16)
            return carry

        lax.fori_loop(0, act_ref.shape[1] // 256, step, 0)

    swaps = []
    for n, bx in ((0, ox), (1, x)):
        multiply(n)
        swap = remote(
            part_ref.at[bx * 2 + oc], near.at[n], near_send.at[n], near_recv.at[n], lat, pair
        )
        swap.start()
        swaps.append(swap)
    multiply(2)
    swaps[0].wait_recv()
    cuts = [pl.ds(n * half, half) for n in range(2)]
    outs = []
    for n, cut in enumerate(cuts):
        sent[cut, :] = (
            part_ref[across, cut, :].astype(f32) + near[0, cut, :].astype(f32)
        ).astype(bf16)
        move = remote(
            sent.at[cut], far.at[cut], far_send.at[n], far_recv.at[n], lat, across
        )
        move.start()
        outs.append(move)
    multiply(3)
    swaps[1].wait_recv()
    gives = []
    for n, cut in enumerate(cuts):
        outs[n].wait_recv()
        total = (
            part_ref[tok, cut, :].astype(f32)
            + near[1, cut, :].astype(f32)
            + far[cut, :].astype(f32)
        )
        out_ref[tok, cut, :] = ((total + bias_ref[cut, :]) * active_ref[cut, :]).astype(bf16)
        mine = out_ref.at[tok, cut]
        for give in (
            remote(mine, mine, x_send.at[n], x_recv.at[n], lat, across),
            remote(mine, mine, c_send.at[n], c_recv.at[n], lat, pair),
        ):
            give.start()
            gives.append(give)
    for n, cut in enumerate(cuts):
        got = out_ref.at[across, cut]
        remote(got, got, x_send.at[n], x_recv.at[n], lat, across).wait_recv()
        give = remote(got, got, f_send.at[n], f_recv.at[n], lat, pair)
        give.start()
        gives.append(give)
    for n, cut in enumerate(cuts):
        got = out_ref.at[pair, cut]
        remote(got, got, c_send.at[n], c_recv.at[n], lat, pair).wait_recv()
        got = out_ref.at[ox * 2 + oc, cut]
        remote(got, got, f_send.at[n], f_recv.at[n], lat, pair).wait_recv()
    for move in swaps + outs + gives:
        move.wait_send()


def masked_sum(w, act, bias, active, ident):
    total, tokens = w.shape[0], act.shape[1]
    rows = total // 4
    return call(
        masked_sum_kernel,
        jax.ShapeDtypeStruct((4, rows, tokens), bf16),
        (w.reshape(4, rows, w.shape[1]), act, bias, active),
        [VMEM((4, rows, w.shape[1]), bf16), VMEM((4, rows, tokens), bf16), DMA((4,))]
        + [VMEM((2, rows, tokens), bf16), VMEM((rows, tokens), bf16), VMEM((rows, tokens), bf16)]
        + [DMA((2,))] * 10,
        ident,
        "masked_sum_%d" % ident,
        (0,),
    ).reshape(total, tokens)


def errors_kernel(
    w_ref, codes_ref, bias_ref, resid_ref, out_ref,
    w, part_ref, w_sem, side, below, above, sent,
    side_send, side_recv, line_send, below_recv, above_recv,
    up_send, down_send, turn_send, gather_recv,
):
    lat, tok = lax.axis_index("lat"), lax.axis_index("tok")
    z, y = lat // 2, lat % 2
    oy = 1 - y
    beside = z * 2 + oy
    high = z // 2
    order = (3 - 3 * high, 2 - high, 1 - z + 4 * high, z)
    feats = part_ref.shape[1]
    blocks = [d * 2 + oy for d in order] + [d * 2 + y for d in order]
    loads = []
    for n, block in enumerate(blocks):
        load = pltpu.make_async_copy(
            w_ref.at[:, pl.ds(pl.multiple_of(block * feats, feats), feats)], w.at[n], w_sem.at[n]
        )
        load.start()
        loads.append(load)
    greet(column(lat, tok, 8))

    def multiply(n):
        loads[n].wait()

        def step(m, carry):
            cols = pl.ds(pl.multiple_of(m * 256, 256), 256)
            part_ref[blocks[n], :, cols] = lax.dot_general(
                w[n], codes_ref[:, cols], (((0,), (0,)), ((), ())), preferred_element_type=f32
            ).astype(bf16)
            return carry

        lax.fori_loop(0, codes_ref.shape[1] // 256, step, 0)

    swaps = []
    for n, d in enumerate(order):
        multiply(n)
        swap = remote(
            part_ref.at[d * 2 + oy], side.at[d], side_send.at[d], side_recv.at[d], beside, tok
        )
        swap.start()
        swaps.append(swap)

    def held(d):
        return part_ref[d * 2 + y].astype(f32) + side[d].astype(f32)

    lines = []
    for n, (d, swap) in enumerate(zip(order[:3], swaps[:3])):
        multiply(4 + n)
        swap.wait_recv()
        up = remote(sent.at[d], below.at[d], line_send.at[d], below_recv.at[d], lat + 2, tok)
        down = remote(sent.at[d], above.at[d], line_send.at[d], above_recv.at[d], lat - 2, tok)
        sent[d] = held(d).astype(bf16)

        @pl.when(jnp.logical_and(d > z, z > 0))
        def _():
            up.wait_recv()
            sent[d] = (held(d) + below[d].astype(f32)).astype(bf16)

        @pl.when(jnp.logical_and(d < z, z < 3))
        def _():
            down.wait_recv()
            sent[d] = (held(d) + above[d].astype(f32)).astype(bf16)

        @pl.when(d > z)
        def _():
            up.start()

        @pl.when(d < z)
        def _():
            down.start()

        lines.append((d, up, down))
    multiply(7)
    swaps[3].wait_recv()

    from_below = remote(sent.at[z], below.at[z], line_send.at[z], below_recv.at[z], lat, tok)
    from_above = remote(sent.at[z], above.at[z], line_send.at[z], above_recv.at[z], lat, tok)

    def finish(total):
        out_ref[lat] = (total + bias_ref[...] - resid_ref[...].astype(f32)).astype(bf16)

    @pl.when(z == 0)
    def _():
        from_above.wait_recv()
        finish(held(z) + above[z].astype(f32))

    @pl.when(z == 3)
    def _():
        from_below.wait_recv()
        finish(held(z) + below[z].astype(f32))

    @pl.when(jnp.logical_and(z > 0, z < 3))
    def _():
        from_below.wait_recv()
        from_above.wait_recv()
        finish(held(z) + below[z].astype(f32) + above[z].astype(f32))

    def relay(o):
        here = out_ref.at[o * 2 + y]
        arrived = gather_recv.at[o * 2 + y]
        return (
            remote(here, here, up_send.at[o], arrived, lat + 2, tok),
            remote(here, here, down_send.at[o], arrived, lat - 2, tok),
            remote(here, here, turn_send.at[o], arrived, beside, tok),
        )

    up, down, turn = relay(z)
    pl.when(z < 3)(up.start)
    pl.when(z > 0)(down.start)
    turn.start()
    for s in range(1, 4):
        @pl.when(z - s >= 0)
        def _():
            up, down, turn = relay(z - s)
            turn.wait_recv()
            pl.when(z < 3)(up.start)
            turn.start()

        @pl.when(z + s <= 3)
        def _():
            up, down, turn = relay(z + s)
            turn.wait_recv()
            pl.when(z > 0)(down.start)
            turn.start()

    for o in range(4):
        there = out_ref.at[o * 2 + oy]
        remote(there, there, turn_send.at[o], gather_recv.at[o * 2 + oy], beside, tok).wait_recv()
    for o in range(4):
        up, down, turn = relay(o)
        pl.when(jnp.logical_and(o <= z, z < 3))(up.wait_send)
        pl.when(jnp.logical_and(o >= z, z > 0))(down.wait_send)
        turn.wait_send()
    for swap in swaps:
        swap.wait_send()
    for d, up, down in lines:
        up.wait_send()


def errors_of(w, codes, bias, resid_rows):
    total, tokens = w.shape[1], codes.shape[1]
    rows = total // 8
    return call(
        errors_kernel,
        jax.ShapeDtypeStruct((8, rows, tokens), bf16),
        (w, codes, bias, resid_rows),
        [VMEM((8, w.shape[0], rows), bf16), VMEM((8, rows, tokens), bf16), DMA((8,))]
        + [VMEM((4, rows, tokens), bf16)] * 4 + [DMA((4,))] * 8 + [DMA((8,))],
        4,
        "recon_errors",
        (0,),
    ).reshape(total, tokens)


def small_sum_kernel(x_ref, out_ref, held, send, recv):
    lat, tok = lax.axis_index("lat"), lax.axis_index("tok")
    greet(column(lat, tok, 8))
    moves = []
    for s in range(1, 8):
        move = remote(
            x_ref, held.at[s], send.at[s], recv.at[s], lax.rem(lat + s, 8), tok
        )
        move.start()
        moves.append(move)
    held[0] = x_ref[...]
    for move in moves:
        move.wait_recv()
    out_ref[...] = jnp.sum(held[...], axis=0)
    for move in moves:
        move.wait_send()


def small_sum(x):
    wide = x.reshape(x.shape[0] // 128, 128)
    return call(
        small_sum_kernel,
        jax.ShapeDtypeStruct(wide.shape, f32),
        (wide,),
        [VMEM((8,) + wide.shape, f32), DMA((8,)), DMA((8,))],
        5,
        "small_sum",
    ).reshape(x.shape)


def active_rows(ids, base, rows):
    word = 32 if rows % 32 == 0 else rows
    local = ids - base
    which = local // word
    place = local - which * word
    bit = lax.shift_left(jnp.int32(1), place)
    words = lax.iota(jnp.int32, rows // word)
    held = jnp.where(which[None, :, :] == words[:, None, None], bit[None, :, :], 0)
    held = jnp.sum(held, axis=1)
    shifts = lax.iota(jnp.int32, word)
    flags = lax.shift_right_logical(held[:, None, :], jnp.broadcast_to(shifts[None, :, None], (rows // word, word, held.shape[1]))) & 1
    return flags.reshape(rows, held.shape[1]).astype(f32)


def on_device(kernels, resid, active_ids, w_enc, w_dec, b_enc, b_dec):
    block_rows = w_enc.shape[0]
    width = w_enc.shape[1]
    lat_pos = lax.axis_index("lat")
    tok_pos = lax.axis_index("tok")
    tok_count = lax.axis_size("tok")
    lat_count = lax.axis_size("lat")
    rows = block_rows // tok_count
    feats = width // lat_count

    if kernels:
        resid_mine, bias_mine, ids_all = spread(resid, b_dec, active_ids)
    else:
        ids_all = lax.all_gather(active_ids, "tok", axis=0, tiled=True).T
        bias_full = lax.all_gather(b_dec, "lat", axis=0, tiled=True)
        resid_full = lax.all_gather(resid, "lat", axis=0, tiled=True)
        resid_mine = lax.all_to_all(resid_full, "tok", split_axis=0, concat_axis=1, tiled=True)
        bias_mine = lax.dynamic_slice_in_dim(bias_full, tok_pos * width, width, 0).astype(f32)
    centred = (resid_mine.astype(f32) - bias_mine[:, None]).astype(bf16)

    active = active_rows(ids_all, lat_pos * block_rows + tok_pos * rows, rows)
    b_rows = lax.dynamic_slice_in_dim(b_enc, tok_pos * rows, rows, 0)

    if kernels:
        codes = masked_sum(w_enc, centred, b_rows[:, None], active, 2)
    else:
        pre_part = jnp.dot(w_enc, centred, preferred_element_type=f32)
        pre = lax.psum_scatter(pre_part, "tok", scatter_dimension=0, tiled=True)
        codes_rows = ((pre + b_rows[:, None]) * active).astype(bf16)
        codes = lax.all_gather(codes_rows, "tok", axis=0, tiled=True)

    r_rows = lax.dynamic_slice_in_dim(resid_mine, lat_pos * feats, feats, 0)
    bd_rows = lax.dynamic_slice_in_dim(bias_mine, lat_pos * feats, feats, 0)
    bd_rows = bd_rows[:, None]
    if kernels:
        errors = errors_of(w_dec, codes, bd_rows, r_rows)
    else:
        recon_part = lax.dot_general(
            w_dec, codes, (((0,), (0,)), ((), ())), preferred_element_type=f32
        )
        recon = lax.psum_scatter(recon_part, "lat", scatter_dimension=0, tiled=True)
        error_rows = (recon + bd_rows - r_rows.astype(f32)).astype(bf16)
        errors = lax.all_gather(error_rows, "lat", axis=0, tiled=True)

    if kernels:
        grad_pre = masked_sum(w_dec, errors, jnp.zeros((rows, 1), f32), active, 3)
    else:
        gc_part = jnp.dot(w_dec, errors, preferred_element_type=f32)
        gc = lax.psum_scatter(gc_part, "tok", scatter_dimension=0, tiled=True)
        gp_rows = (gc * active).astype(bf16)
        grad_pre = lax.all_gather(gp_rows, "tok", axis=0, tiled=True)

    grad_w_dec = lax.dot_general(
        codes, errors, (((1,), (1,)), ((), ())), preferred_element_type=f32
    ).astype(bf16)
    grad_b_enc = jnp.sum(grad_pre.astype(f32), axis=1)
    high = grad_b_enc.astype(bf16)
    rest = grad_b_enc - high.astype(f32)
    mid = rest.astype(bf16)
    low = (rest - mid.astype(f32)).astype(bf16)
    parts = jnp.stack([high, mid, low])
    back = jnp.sum(jnp.dot(parts, w_enc, preferred_element_type=f32), axis=0)
    back = small_sum(back) if kernels else lax.psum(back, "lat")
    error_total = jnp.sum(errors.astype(f32), axis=1)
    grad_w_enc = lax.dot_general(
        grad_pre, centred, (((1,), (1,)), ((), ())), preferred_element_type=f32
    ).astype(bf16)
    return (grad_w_enc, grad_w_dec, grad_b_enc, error_total - back)


def solution(mesh):
    kernels = mesh.shape["lat"] == 8 and mesh.shape["tok"] == 4
    return jax.shard_map(
        functools.partial(on_device, kernels),
        mesh=mesh,
        in_specs=(
            P("lat", "tok"),
            P("tok", None),
            P("lat", "tok"),
            P("lat", "tok"),
            P("lat"),
            P("lat"),
        ),
        out_specs=(P("lat", "tok"), P("lat", "tok"), P("lat"), P("tok")),
        check_vma=False,
    )
```

```python
import functools

import jax
import jax.numpy as jnp
from jax import lax
from jax.experimental import pallas as pl
from jax.experimental.pallas import tpu as pltpu
from jax.sharding import PartitionSpec as P

f32 = jnp.float32
bf16 = jnp.bfloat16
MESH = pl.DeviceIdType.MESH
DMA = pltpu.SemaphoreType.DMA
VMEM = pltpu.VMEM


def remote(src, dst, send, recv, lat, tok):
    return pltpu.make_async_remote_copy(
        src_ref=src, dst_ref=dst, send_sem=send, recv_sem=recv,
        device_id=(lat, tok), device_id_type=MESH,
    )


def greet(devices):
    barrier = pltpu.get_barrier_semaphore()
    for lat, tok in devices:
        pl.semaphore_signal(barrier, inc=1, device_id=(lat, tok), device_id_type=MESH)
    pl.semaphore_wait(barrier, len(devices))


def column(lat, tok, count):
    return [(lax.rem(lat + s, count), tok) for s in range(1, count)]


def group(lat, tok, count):
    return [(lat, lax.rem(tok + s, count)) for s in range(1, count)]


def call(kernel, out_shape, inputs, scratch, ident, name, whole=()):
    return pl.pallas_call(
        kernel,
        out_shape=out_shape,
        in_specs=[
            pl.BlockSpec(memory_space=pl.ANY if n in whole else VMEM)
            for n in range(len(inputs))
        ],
        out_specs=jax.tree.map(lambda _: pl.BlockSpec(memory_space=VMEM), out_shape),
        scratch_shapes=scratch,
        compiler_params=pltpu.CompilerParams(
            collective_id=ident, has_side_effects=True, vmem_limit_bytes=44 * 2**20
        ),
        name=name,
    )(*inputs)


def spread_kernel(
    x_ref, bias_ref, ids_ref, out_ref, bias_out, ids_out,
    own_sem, first_send, up_send, down_send, side_send, recv,
    bias_send, bias_recv, ids_send, ids_recv,
):
    lat, tok = lax.axis_index("lat"), lax.axis_index("tok")
    z, y = lat // 2, lat % 2
    rows, cols = x_ref.shape
    pieces = 2
    cut = rows // pieces
    greet(column(lat, tok, 8) + group(lat, tok, 4))

    def place(half, part, n):
        return out_ref.at[
            pl.ds(pl.multiple_of(half * rows + n * cut, cut), cut),
            pl.ds(pl.multiple_of(part * cols, cols), cols),
        ]

    def sem_of(half, part, n):
        return recv.at[half * (4 * pieces) + part * pieces + n]

    firsts = []
    for n in range(pieces):
        mine = x_ref.at[pl.ds(n * cut, cut)]
        home = remote(mine, place(y, tok, n), first_send.at[n], sem_of(y, tok, n), lat, z)
        own = pltpu.make_async_copy(mine, place(y, tok, n), own_sem.at[n])
        pl.when(tok != z)(home.start)
        pl.when(tok == z)(own.start)
        firsts.append((home, own))

    bias_moves = [
        remote(bias_ref, bias_out.at[y], bias_send.at[s], bias_recv.at[y], lax.rem(lat + s, 8), tok)
        for s in range(1, 8)
    ]

    @pl.when(tok == z)
    def _():
        for move in bias_moves:
            move.start()
        bias_out[y] = bias_ref[...]

    def ids_place(part):
        return ids_out.at[:, pl.ds(pl.multiple_of(part * cols, cols), cols)]

    ids_moves = []
    for s in range(1, 4):
        move = remote(
            ids_ref, ids_place(tok), ids_send.at[s], ids_recv.at[s], lat, lax.rem(tok + s, 4)
        )
        move.start()
        ids_moves.append(move)
    ids_out[:, pl.ds(pl.multiple_of(tok * cols, cols), cols)] = ids_ref[...]

    goes_up = jnp.logical_and(z >= tok, z < 3)
    goes_down = jnp.logical_and(z <= tok, z > 0)
    moves = []
    for k in range(4):
        part = lax.rem(tok + k, 4)
        for n in range(pieces):
            m = k * pieces + n
            here = place(y, part, n)
            arrived = sem_of(y, part, n)
            up = remote(here, here, up_send.at[m], arrived, lat + 2, tok)
            down = remote(here, here, down_send.at[m], arrived, lat - 2, tok)
            side = remote(here, here, side_send.at[m], arrived, lat + 1 - 2 * y, tok)
            if k == 0:
                pl.when(tok == z)(firsts[n][1].wait)
                pl.when(tok != z)(side.wait_recv)
            else:
                side.wait_recv()
            pl.when(goes_up)(up.start)
            pl.when(goes_down)(down.start)
            side.start()
            moves.append((up, down, side))
    for k in range(4):
        part = lax.rem(tok + k, 4)
        for n in range(pieces):
            there = place(1 - y, part, n)
            remote(
                there, there, side_send.at[0], sem_of(1 - y, part, n), lat, tok
            ).wait_recv()
    for h in range(2):
        @pl.when(jnp.logical_or(tok != z, y != h))
        def _():
            remote(
                bias_ref, bias_out.at[h], bias_send.at[0], bias_recv.at[h], lat, tok
            ).wait_recv()
    for move in ids_moves:
        move.wait_recv()
        move.wait_send()
    for up, down, side in moves:
        pl.when(goes_up)(up.wait_send)
        pl.when(goes_down)(down.wait_send)
        side.wait_send()
    for home, own in firsts:
        pl.when(tok != z)(home.wait_send)

    @pl.when(tok == z)
    def _():
        for move in bias_moves:
            move.wait_send()


def spread(resid, bias, ids):
    rows, cols = resid.shape
    wide = bias.astype(f32).reshape(rows // 128, 128)
    resid_mine, bias_mine, ids_all = call(
        spread_kernel,
        (
            jax.ShapeDtypeStruct((2 * rows, 4 * cols), resid.dtype),
            jax.ShapeDtypeStruct((2,) + wide.shape, f32),
            jax.ShapeDtypeStruct((ids.shape[1], 4 * cols), ids.dtype),
        ),
        (resid, wide, ids.T),
        [DMA((2,)), DMA((2,)), DMA((8,)), DMA((8,)), DMA((8,)), DMA((16,))]
        + [DMA((8,)), DMA((2,)), DMA((4,)), DMA((4,))],
        1,
        "spread_features",
    )
    return resid_mine, bias_mine.reshape(2 * rows), ids_all


def masked_sum_kernel(
    w_ref, act_ref, bias_ref, active_ref, out_ref,
    w, part_ref, w_sem, near, sent, far, near_send, near_recv, far_send, far_recv,
    x_send, x_recv, c_send, c_recv, f_send, f_recv,
):
    lat, tok = lax.axis_index("lat"), lax.axis_index("tok")
    x, c = tok // 2, tok % 2
    ox, oc = 1 - x, 1 - c
    pair, across = x * 2 + oc, ox * 2 + c
    rows = part_ref.shape[1]
    half = rows // 2
    order = (ox * 2 + oc, pair, across, tok)
    loads = []
    for n, block in enumerate(order):
        load = pltpu.make_async_copy(w_ref.at[block], w.at[n], w_sem.at[n])
        load.start()
        loads.append(load)
    greet([(lat, pair), (lat, across)])

    def multiply(n):
        loads[n].wait()

        def step(m, carry):
            cols = pl.ds(pl.multiple_of(m * 256, 256), 256)
            part_ref[order[n], :, cols] = jnp.dot(
                w[n], act_ref[:, cols], preferred_element_type=f32
            ).astype(bf16)
            return carry

        lax.fori_loop(0, act_ref.shape[1] // 256, step, 0)

    swaps = []
    for n, bx in ((0, ox), (1, x)):
        multiply(n)
        swap = remote(
            part_ref.at[bx * 2 + oc], near.at[n], near_send.at[n], near_recv.at[n], lat, pair
        )
        swap.start()
        swaps.append(swap)
    multiply(2)
    swaps[0].wait_recv()
    cuts = [pl.ds(n * half, half) for n in range(2)]
    outs = []
    for n, cut in enumerate(cuts):
        sent[cut, :] = (
            part_ref[across, cut, :].astype(f32) + near[0, cut, :].astype(f32)
        ).astype(bf16)
        move = remote(
            sent.at[cut], far.at[cut], far_send.at[n], far_recv.at[n], lat, across
        )
        move.start()
        outs.append(move)
    multiply(3)
    swaps[1].wait_recv()
    gives = []
    for n, cut in enumerate(cuts):
        outs[n].wait_recv()
        total = (
            part_ref[tok, cut, :].astype(f32)
            + near[1, cut, :].astype(f32)
            + far[cut, :].astype(f32)
        )
        out_ref[tok, cut, :] = ((total + bias_ref[cut, :]) * active_ref[cut, :]).astype(bf16)
        mine = out_ref.at[tok, cut]
        for give in (
            remote(mine, mine, x_send.at[n], x_recv.at[n], lat, across),
            remote(mine, mine, c_send.at[n], c_recv.at[n], lat, pair),
        ):
            give.start()
            gives.append(give)
    for n, cut in enumerate(cuts):
        got = out_ref.at[across, cut]
        remote(got, got, x_send.at[n], x_recv.at[n], lat, across).wait_recv()
        give = remote(got, got, f_send.at[n], f_recv.at[n], lat, pair)
        give.start()
        gives.append(give)
    for n, cut in enumerate(cuts):
        got = out_ref.at[pair, cut]
        remote(got, got, c_send.at[n], c_recv.at[n], lat, pair).wait_recv()
        got = out_ref.at[ox * 2 + oc, cut]
        remote(got, got, f_send.at[n], f_recv.at[n], lat, pair).wait_recv()
    for move in swaps + outs + gives:
        move.wait_send()


def masked_sum(w, act, bias, active, ident):
    total, tokens = w.shape[0], act.shape[1]
    rows = total // 4
    return call(
        masked_sum_kernel,
        jax.ShapeDtypeStruct((4, rows, tokens), bf16),
        (w.reshape(4, rows, w.shape[1]), act, bias, active),
        [VMEM((4, rows, w.shape[1]), bf16), VMEM((4, rows, tokens), bf16), DMA((4,))]
        + [VMEM((2, rows, tokens), bf16), VMEM((rows, tokens), bf16), VMEM((rows, tokens), bf16)]
        + [DMA((2,))] * 10,
        ident,
        "masked_sum_%d" % ident,
        (0,),
    ).reshape(total, tokens)


def errors_kernel(
    w_ref, codes_ref, bias_ref, resid_ref, out_ref,
    w, part_ref, w_sem, side, below, above, sent,
    side_send, side_recv, line_send, below_recv, above_recv,
    up_send, down_send, turn_send, gather_recv,
):
    lat, tok = lax.axis_index("lat"), lax.axis_index("tok")
    z, y = lat // 2, lat % 2
    oy = 1 - y
    beside = z * 2 + oy
    high = z // 2
    order = (3 - 3 * high, 2 - high, 1 - z + 4 * high, z)
    feats = part_ref.shape[1]
    blocks = [d * 2 + oy for d in order] + [d * 2 + y for d in order]
    loads = []
    for n, block in enumerate(blocks):
        load = pltpu.make_async_copy(
            w_ref.at[:, pl.ds(pl.multiple_of(block * feats, feats), feats)], w.at[n], w_sem.at[n]
        )
        load.start()
        loads.append(load)
    greet(column(lat, tok, 8))

    width = codes_ref.shape[1] // 2

    def multiply(n, h):
        if h == 0:
            loads[n].wait()
        cols = pl.ds(h * width, width)
        part_ref[blocks[n], :, cols] = lax.dot_general(
            w[n], codes_ref[:, cols], (((0,), (0,)), ((), ())), preferred_element_type=f32
        ).astype(bf16)

    swaps = []
    for h in range(2):
        cols = pl.ds(h * width, width)
        for n, d in enumerate(order):
            multiply(n, h)
            swap = remote(
                part_ref.at[d * 2 + oy, :, cols], side.at[d, :, cols],
                side_send.at[h * 4 + d], side_recv.at[h * 4 + d], beside, tok,
            )
            swap.start()
            swaps.append(swap)

    lines = []

    def reduce(h):
        cols = pl.ds(h * width, width)

        def held(d):
            return part_ref[d * 2 + y, :, cols].astype(f32) + side[d, :, cols].astype(f32)

        def chain(d):
            m = h * 4 + d
            src = sent.at[d, :, cols]
            return (
                remote(src, below.at[d, :, cols], line_send.at[m], below_recv.at[m], lat + 2, tok),
                remote(src, above.at[d, :, cols], line_send.at[m], above_recv.at[m], lat - 2, tok),
            )

        for n, d in enumerate(order[:3]):
            multiply(4 + n, h)
            swaps[h * 4 + n].wait_recv()
            up, down = chain(d)
            sent[d, :, cols] = held(d).astype(bf16)

            @pl.when(jnp.logical_and(d > z, z > 0))
            def _():
                up.wait_recv()
                sent[d, :, cols] = (held(d) + below[d, :, cols].astype(f32)).astype(bf16)

            @pl.when(jnp.logical_and(d < z, z < 3))
            def _():
                down.wait_recv()
                sent[d, :, cols] = (held(d) + above[d, :, cols].astype(f32)).astype(bf16)

            pl.when(d > z)(up.start)
            pl.when(d < z)(down.start)
            lines.append(up)
        multiply(7, h)
        swaps[h * 4 + 3].wait_recv()
        from_below, from_above = chain(z)

        def finish(total):
            out_ref[lat, :, cols] = (
                total + bias_ref[...] - resid_ref[:, cols].astype(f32)
            ).astype(bf16)

        @pl.when(z == 0)
        def _():
            from_above.wait_recv()
            finish(held(z) + above[z, :, cols].astype(f32))

        @pl.when(z == 3)
        def _():
            from_below.wait_recv()
            finish(held(z) + below[z, :, cols].astype(f32))

        @pl.when(jnp.logical_and(z > 0, z < 3))
        def _():
            from_below.wait_recv()
            from_above.wait_recv()
            finish(
                held(z) + below[z, :, cols].astype(f32) + above[z, :, cols].astype(f32)
            )

    def relay(o, h):
        here = out_ref.at[o * 2 + y, :, pl.ds(h * width, width)]
        arrived = gather_recv.at[h * 8 + o * 2 + y]
        m = h * 4 + o
        return (
            remote(here, here, up_send.at[m], arrived, lat + 2, tok),
            remote(here, here, down_send.at[m], arrived, lat - 2, tok),
            remote(here, here, turn_send.at[m], arrived, beside, tok),
        )

    for h in range(2):
        reduce(h)
        up, down, turn = relay(z, h)
        pl.when(z < 3)(up.start)
        pl.when(z > 0)(down.start)
        turn.start()
    for h in range(2):
        for s in range(1, 4):
            @pl.when(z - s >= 0)
            def _():
                up, down, turn = relay(z - s, h)
                turn.wait_recv()
                pl.when(z < 3)(up.start)
                turn.start()

            @pl.when(z + s <= 3)
            def _():
                up, down, turn = relay(z + s, h)
                turn.wait_recv()
                pl.when(z > 0)(down.start)
                turn.start()

    for h in range(2):
        for o in range(4):
            there = out_ref.at[o * 2 + oy, :, pl.ds(h * width, width)]
            arrived = gather_recv.at[h * 8 + o * 2 + oy]
            remote(there, there, turn_send.at[h * 4 + o], arrived, beside, tok).wait_recv()
    for h in range(2):
        for o in range(4):
            up, down, turn = relay(o, h)
            pl.when(jnp.logical_and(o <= z, z < 3))(up.wait_send)
            pl.when(jnp.logical_and(o >= z, z > 0))(down.wait_send)
            turn.wait_send()
    for move in swaps + lines:
        move.wait_send()


def errors_of(w, codes, bias, resid_rows):
    total, tokens = w.shape[1], codes.shape[1]
    rows = total // 8
    return call(
        errors_kernel,
        jax.ShapeDtypeStruct((8, rows, tokens), bf16),
        (w, codes, bias, resid_rows),
        [VMEM((8, w.shape[0], rows), bf16), VMEM((8, rows, tokens), bf16), DMA((8,))]
        + [VMEM((4, rows, tokens), bf16)] * 4 + [DMA((8,))] * 8 + [DMA((16,))],
        4,
        "recon_errors",
        (0,),
    ).reshape(total, tokens)


def small_sum_kernel(x_ref, out_ref, held, send, recv):
    lat, tok = lax.axis_index("lat"), lax.axis_index("tok")
    greet(column(lat, tok, 8))
    moves = []
    for s in range(1, 8):
        move = remote(
            x_ref, held.at[s], send.at[s], recv.at[s], lax.rem(lat + s, 8), tok
        )
        move.start()
        moves.append(move)
    held[0] = x_ref[...]
    for move in moves:
        move.wait_recv()
    out_ref[...] = jnp.sum(held[...], axis=0)
    for move in moves:
        move.wait_send()


def small_sum(x):
    wide = x.reshape(x.shape[0] // 128, 128)
    return call(
        small_sum_kernel,
        jax.ShapeDtypeStruct(wide.shape, f32),
        (wide,),
        [VMEM((8,) + wide.shape, f32), DMA((8,)), DMA((8,))],
        5,
        "small_sum",
    ).reshape(x.shape)


def active_rows(ids, base, rows):
    word = 32 if rows % 32 == 0 else rows
    local = ids - base
    which = local // word
    place = local - which * word
    bit = lax.shift_left(jnp.int32(1), place)
    words = lax.iota(jnp.int32, rows // word)
    held = jnp.where(which[None, :, :] == words[:, None, None], bit[None, :, :], 0)
    held = jnp.sum(held, axis=1)
    shifts = lax.iota(jnp.int32, word)
    flags = lax.shift_right_logical(held[:, None, :], jnp.broadcast_to(shifts[None, :, None], (rows // word, word, held.shape[1]))) & 1
    return flags.reshape(rows, held.shape[1]).astype(f32)


def on_device(kernels, resid, active_ids, w_enc, w_dec, b_enc, b_dec):
    block_rows = w_enc.shape[0]
    width = w_enc.shape[1]
    lat_pos = lax.axis_index("lat")
    tok_pos = lax.axis_index("tok")
    tok_count = lax.axis_size("tok")
    lat_count = lax.axis_size("lat")
    rows = block_rows // tok_count
    feats = width // lat_count

    if kernels:
        resid_mine, bias_mine, ids_all = spread(resid, b_dec, active_ids)
    else:
        ids_all = lax.all_gather(active_ids, "tok", axis=0, tiled=True).T
        bias_full = lax.all_gather(b_dec, "lat", axis=0, tiled=True)
        resid_full = lax.all_gather(resid, "lat", axis=0, tiled=True)
        resid_mine = lax.all_to_all(resid_full, "tok", split_axis=0, concat_axis=1, tiled=True)
        bias_mine = lax.dynamic_slice_in_dim(bias_full, tok_pos * width, width, 0).astype(f32)
    centred = (resid_mine.astype(f32) - bias_mine[:, None]).astype(bf16)

    active = active_rows(ids_all, lat_pos * block_rows + tok_pos * rows, rows)
    b_rows = lax.dynamic_slice_in_dim(b_enc, tok_pos * rows, rows, 0)

    if kernels:
        codes = masked_sum(w_enc, centred, b_rows[:, None], active, 2)
    else:
        pre_part = jnp.dot(w_enc, centred, preferred_element_type=f32)
        pre = lax.psum_scatter(pre_part, "tok", scatter_dimension=0, tiled=True)
        codes_rows = ((pre + b_rows[:, None]) * active).astype(bf16)
        codes = lax.all_gather(codes_rows, "tok", axis=0, tiled=True)

    r_rows = lax.dynamic_slice_in_dim(resid_mine, lat_pos * feats, feats, 0)
    bd_rows = lax.dynamic_slice_in_dim(bias_mine, lat_pos * feats, feats, 0)
    bd_rows = bd_rows[:, None]
    if kernels:
        errors = errors_of(w_dec, codes, bd_rows, r_rows)
    else:
        recon_part = lax.dot_general(
            w_dec, codes, (((0,), (0,)), ((), ())), preferred_element_type=f32
        )
        recon = lax.psum_scatter(recon_part, "lat", scatter_dimension=0, tiled=True)
        error_rows = (recon + bd_rows - r_rows.astype(f32)).astype(bf16)
        errors = lax.all_gather(error_rows, "lat", axis=0, tiled=True)

    if kernels:
        grad_pre = masked_sum(w_dec, errors, jnp.zeros((rows, 1), f32), active, 3)
    else:
        gc_part = jnp.dot(w_dec, errors, preferred_element_type=f32)
        gc = lax.psum_scatter(gc_part, "tok", scatter_dimension=0, tiled=True)
        gp_rows = (gc * active).astype(bf16)
        grad_pre = lax.all_gather(gp_rows, "tok", axis=0, tiled=True)

    grad_w_dec = lax.dot_general(
        codes, errors, (((1,), (1,)), ((), ())), preferred_element_type=f32
    ).astype(bf16)
    grad_b_enc = jnp.sum(grad_pre.astype(f32), axis=1)
    high = grad_b_enc.astype(bf16)
    rest = grad_b_enc - high.astype(f32)
    mid = rest.astype(bf16)
    low = (rest - mid.astype(f32)).astype(bf16)
    parts = jnp.stack([high, mid, low])
    back = jnp.sum(jnp.dot(parts, w_enc, preferred_element_type=f32), axis=0)
    back = small_sum(back) if kernels else lax.psum(back, "lat")
    error_total = jnp.sum(errors.astype(f32), axis=1)
    grad_w_enc = lax.dot_general(
        grad_pre, centred, (((1,), (1,)), ((), ())), preferred_element_type=f32
    ).astype(bf16)
    return (grad_w_enc, grad_w_dec, grad_b_enc, error_total - back)


def solution(mesh):
    kernels = mesh.shape["lat"] == 8 and mesh.shape["tok"] == 4
    return jax.shard_map(
        functools.partial(on_device, kernels),
        mesh=mesh,
        in_specs=(
            P("lat", "tok"),
            P("tok", None),
            P("lat", "tok"),
            P("lat", "tok"),
            P("lat"),
            P("lat"),
        ),
        out_specs=(P("lat", "tok"), P("lat", "tok"), P("lat"), P("tok")),
        check_vma=False,
    )
```

```python
import functools

import jax
import jax.numpy as jnp
from jax import lax
from jax.experimental import pallas as pl
from jax.experimental.pallas import tpu as pltpu
from jax.sharding import PartitionSpec as P

f32 = jnp.float32
bf16 = jnp.bfloat16
MESH = pl.DeviceIdType.MESH
DMA = pltpu.SemaphoreType.DMA
VMEM = pltpu.VMEM


def remote(src, dst, send, recv, lat, tok):
    return pltpu.make_async_remote_copy(
        src_ref=src, dst_ref=dst, send_sem=send, recv_sem=recv,
        device_id=(lat, tok), device_id_type=MESH,
    )


def greet(devices):
    barrier = pltpu.get_barrier_semaphore()
    for lat, tok in devices:
        pl.semaphore_signal(barrier, inc=1, device_id=(lat, tok), device_id_type=MESH)
    pl.semaphore_wait(barrier, len(devices))


def column(lat, tok, count):
    return [(lax.rem(lat + s, count), tok) for s in range(1, count)]


def group(lat, tok, count):
    return [(lat, lax.rem(tok + s, count)) for s in range(1, count)]


def call(kernel, out_shape, inputs, scratch, ident, name, whole=()):
    return pl.pallas_call(
        kernel,
        out_shape=out_shape,
        in_specs=[
            pl.BlockSpec(memory_space=pl.ANY if n in whole else VMEM)
            for n in range(len(inputs))
        ],
        out_specs=jax.tree.map(lambda _: pl.BlockSpec(memory_space=VMEM), out_shape),
        scratch_shapes=scratch,
        compiler_params=pltpu.CompilerParams(
            collective_id=ident, has_side_effects=True, vmem_limit_bytes=44 * 2**20
        ),
        name=name,
    )(*inputs)


def spread_kernel(
    x_ref, bias_ref, ids_ref, out_ref, bias_out, ids_out,
    own_sem, first_send, up_send, down_send, side_send, recv,
    bias_send, bias_recv, ids_send, ids_recv,
):
    lat, tok = lax.axis_index("lat"), lax.axis_index("tok")
    z, y = lat // 2, lat % 2
    rows, cols = x_ref.shape
    pieces = 2
    cut = rows // pieces
    greet(column(lat, tok, 8) + group(lat, tok, 4))

    def place(half, part, n):
        return out_ref.at[
            pl.ds(pl.multiple_of(half * rows + n * cut, cut), cut),
            pl.ds(pl.multiple_of(part * cols, cols), cols),
        ]

    def sem_of(half, part, n):
        return recv.at[half * (4 * pieces) + part * pieces + n]

    firsts = []
    for n in range(pieces):
        mine = x_ref.at[pl.ds(n * cut, cut)]
        home = remote(mine, place(y, tok, n), first_send.at[n], sem_of(y, tok, n), lat, z)
        own = pltpu.make_async_copy(mine, place(y, tok, n), own_sem.at[n])
        pl.when(tok != z)(home.start)
        pl.when(tok == z)(own.start)
        firsts.append((home, own))

    bias_moves = [
        remote(bias_ref, bias_out.at[y], bias_send.at[s], bias_recv.at[y], lax.rem(lat + s, 8), tok)
        for s in range(1, 8)
    ]

    @pl.when(tok == z)
    def _():
        for move in bias_moves:
            move.start()
        bias_out[y] = bias_ref[...]

    def ids_place(part):
        return ids_out.at[:, pl.ds(pl.multiple_of(part * cols, cols), cols)]

    ids_moves = []
    for s in range(1, 4):
        move = remote(
            ids_ref, ids_place(tok), ids_send.at[s], ids_recv.at[s], lat, lax.rem(tok + s, 4)
        )
        move.start()
        ids_moves.append(move)
    ids_out[:, pl.ds(pl.multiple_of(tok * cols, cols), cols)] = ids_ref[...]

    goes_up = jnp.logical_and(z >= tok, z < 3)
    goes_down = jnp.logical_and(z <= tok, z > 0)
    moves = []
    for k in range(4):
        part = lax.rem(tok + k, 4)
        for n in range(pieces):
            m = k * pieces + n
            here = place(y, part, n)
            arrived = sem_of(y, part, n)
            up = remote(here, here, up_send.at[m], arrived, lat + 2, tok)
            down = remote(here, here, down_send.at[m], arrived, lat - 2, tok)
            side = remote(here, here, side_send.at[m], arrived, lat + 1 - 2 * y, tok)
            if k == 0:
                pl.when(tok == z)(firsts[n][1].wait)
                pl.when(tok != z)(side.wait_recv)
            else:
                side.wait_recv()
            pl.when(goes_up)(up.start)
            pl.when(goes_down)(down.start)
            side.start()
            moves.append((up, down, side))
    for k in range(4):
        part = lax.rem(tok + k, 4)
        for n in range(pieces):
            there = place(1 - y, part, n)
            remote(
                there, there, side_send.at[0], sem_of(1 - y, part, n), lat, tok
            ).wait_recv()
    for h in range(2):
        @pl.when(jnp.logical_or(tok != z, y != h))
        def _():
            remote(
                bias_ref, bias_out.at[h], bias_send.at[0], bias_recv.at[h], lat, tok
            ).wait_recv()
    for move in ids_moves:
        move.wait_recv()
        move.wait_send()
    for up, down, side in moves:
        pl.when(goes_up)(up.wait_send)
        pl.when(goes_down)(down.wait_send)
        side.wait_send()
    for home, own in firsts:
        pl.when(tok != z)(home.wait_send)

    @pl.when(tok == z)
    def _():
        for move in bias_moves:
            move.wait_send()


def spread(resid, bias, ids):
    rows, cols = resid.shape
    wide = bias.astype(f32).reshape(rows // 128, 128)
    resid_mine, bias_mine, ids_all = call(
        spread_kernel,
        (
            jax.ShapeDtypeStruct((2 * rows, 4 * cols), resid.dtype),
            jax.ShapeDtypeStruct((2,) + wide.shape, f32),
            jax.ShapeDtypeStruct((ids.shape[1], 4 * cols), ids.dtype),
        ),
        (resid, wide, ids.T),
        [DMA((2,)), DMA((2,)), DMA((8,)), DMA((8,)), DMA((8,)), DMA((16,))]
        + [DMA((8,)), DMA((2,)), DMA((4,)), DMA((4,))],
        1,
        "spread_features",
    )
    return resid_mine, bias_mine.reshape(2 * rows), ids_all


def masked_sum_kernel(
    w_ref, act_ref, bias_ref, active_ref, out_ref,
    w, part_ref, w_sem, near, sent, far, near_send, near_recv, far_send, far_recv,
    x_send, x_recv, c_send, c_recv, f_send, f_recv,
):
    lat, tok = lax.axis_index("lat"), lax.axis_index("tok")
    x, c = tok // 2, tok % 2
    ox, oc = 1 - x, 1 - c
    pair, across = x * 2 + oc, ox * 2 + c
    rows = part_ref.shape[1]
    half = rows // 2
    order = (ox * 2 + oc, pair, across, tok)
    loads = []
    for n, block in enumerate(order):
        load = pltpu.make_async_copy(w_ref.at[block], w.at[n], w_sem.at[n])
        load.start()
        loads.append(load)
    greet([(lat, pair), (lat, across)])

    def multiply(n):
        loads[n].wait()

        def step(m, carry):
            cols = pl.ds(pl.multiple_of(m * 256, 256), 256)
            part_ref[order[n], :, cols] = jnp.dot(
                w[n], act_ref[:, cols], preferred_element_type=f32
            ).astype(bf16)
            return carry

        lax.fori_loop(0, act_ref.shape[1] // 256, step, 0)

    swaps = []
    for n, bx in ((0, ox), (1, x)):
        multiply(n)
        swap = remote(
            part_ref.at[bx * 2 + oc], near.at[n], near_send.at[n], near_recv.at[n], lat, pair
        )
        swap.start()
        swaps.append(swap)
    multiply(2)
    swaps[0].wait_recv()
    cuts = [pl.ds(n * half, half) for n in range(2)]
    outs = []
    for n, cut in enumerate(cuts):
        sent[cut, :] = (
            part_ref[across, cut, :].astype(f32) + near[0, cut, :].astype(f32)
        ).astype(bf16)
        move = remote(
            sent.at[cut], far.at[cut], far_send.at[n], far_recv.at[n], lat, across
        )
        move.start()
        outs.append(move)
    multiply(3)
    swaps[1].wait_recv()
    gives = []
    for n, cut in enumerate(cuts):
        outs[n].wait_recv()
        total = (
            part_ref[tok, cut, :].astype(f32)
            + near[1, cut, :].astype(f32)
            + far[cut, :].astype(f32)
        )
        out_ref[tok, cut, :] = ((total + bias_ref[cut, :]) * active_ref[cut, :]).astype(bf16)
        mine = out_ref.at[tok, cut]
        for give in (
            remote(mine, mine, x_send.at[n], x_recv.at[n], lat, across),
            remote(mine, mine, c_send.at[n], c_recv.at[n], lat, pair),
        ):
            give.start()
            gives.append(give)
    for n, cut in enumerate(cuts):
        got = out_ref.at[across, cut]
        remote(got, got, x_send.at[n], x_recv.at[n], lat, across).wait_recv()
        give = remote(got, got, f_send.at[n], f_recv.at[n], lat, pair)
        give.start()
        gives.append(give)
    for n, cut in enumerate(cuts):
        got = out_ref.at[pair, cut]
        remote(got, got, c_send.at[n], c_recv.at[n], lat, pair).wait_recv()
        got = out_ref.at[ox * 2 + oc, cut]
        remote(got, got, f_send.at[n], f_recv.at[n], lat, pair).wait_recv()
    for move in swaps + outs + gives:
        move.wait_send()


def masked_sum(w, act, bias, active, ident):
    total, tokens = w.shape[0], act.shape[1]
    rows = total // 4
    return call(
        masked_sum_kernel,
        jax.ShapeDtypeStruct((4, rows, tokens), bf16),
        (w.reshape(4, rows, w.shape[1]), act, bias, active),
        [VMEM((4, rows, w.shape[1]), bf16), VMEM((4, rows, tokens), bf16), DMA((4,))]
        + [VMEM((2, rows, tokens), bf16), VMEM((rows, tokens), bf16), VMEM((rows, tokens), bf16)]
        + [DMA((2,))] * 10,
        ident,
        "masked_sum_%d" % ident,
        (0,),
    ).reshape(total, tokens)


def errors_kernel(
    w_ref, codes_ref, bias_ref, resid_ref, out_ref,
    w, part_ref, w_sem, side, below, above, sent,
    side_send, side_recv, line_send, below_recv, above_recv,
    up_send, down_send, turn_send, gather_recv,
):
    lat, tok = lax.axis_index("lat"), lax.axis_index("tok")
    z, y = lat // 2, lat % 2
    oy = 1 - y
    beside = z * 2 + oy
    high = z // 2
    order = (3 - 3 * high, 2 - high, 1 - z + 4 * high, z)
    feats = part_ref.shape[1]
    blocks = [d * 2 + oy for d in order] + [d * 2 + y for d in order]
    loads = []
    for n, block in enumerate(blocks):
        load = pltpu.make_async_copy(
            w_ref.at[:, pl.ds(pl.multiple_of(block * feats, feats), feats)], w.at[n], w_sem.at[n]
        )
        load.start()
        loads.append(load)
    greet(column(lat, tok, 8))

    def multiply(n):
        loads[n].wait()

        def step(m, carry):
            cols = pl.ds(pl.multiple_of(m * 256, 256), 256)
            part_ref[blocks[n], :, cols] = lax.dot_general(
                w[n], codes_ref[:, cols], (((0,), (0,)), ((), ())), preferred_element_type=f32
            ).astype(bf16)
            return carry

        lax.fori_loop(0, codes_ref.shape[1] // 256, step, 0)

    swaps = []
    for n, d in enumerate(order):
        multiply(n)
        swap = remote(
            part_ref.at[d * 2 + oy], side.at[d], side_send.at[d], side_recv.at[d], beside, tok
        )
        swap.start()
        swaps.append(swap)

    def held(d):
        return part_ref[d * 2 + y].astype(f32) + side[d].astype(f32)

    lines = []
    for n, (d, swap) in enumerate(zip(order[:3], swaps[:3])):
        multiply(4 + n)
        swap.wait_recv()
        up = remote(sent.at[d], below.at[d], line_send.at[d], below_recv.at[d], lat + 2, tok)
        down = remote(sent.at[d], above.at[d], line_send.at[d], above_recv.at[d], lat - 2, tok)
        sent[d] = held(d).astype(bf16)

        @pl.when(jnp.logical_and(d > z, z > 0))
        def _():
            up.wait_recv()
            sent[d] = (held(d) + below[d].astype(f32)).astype(bf16)

        @pl.when(jnp.logical_and(d < z, z < 3))
        def _():
            down.wait_recv()
            sent[d] = (held(d) + above[d].astype(f32)).astype(bf16)

        @pl.when(d > z)
        def _():
            up.start()

        @pl.when(d < z)
        def _():
            down.start()

        lines.append((d, up, down))
    multiply(7)
    swaps[3].wait_recv()

    from_below = remote(sent.at[z], below.at[z], line_send.at[z], below_recv.at[z], lat, tok)
    from_above = remote(sent.at[z], above.at[z], line_send.at[z], above_recv.at[z], lat, tok)

    def finish(total):
        out_ref[lat] = (total + bias_ref[...] - resid_ref[...].astype(f32)).astype(bf16)

    @pl.when(z == 0)
    def _():
        from_above.wait_recv()
        finish(held(z) + above[z].astype(f32))

    @pl.when(z == 3)
    def _():
        from_below.wait_recv()
        finish(held(z) + below[z].astype(f32))

    @pl.when(jnp.logical_and(z > 0, z < 3))
    def _():
        from_below.wait_recv()
        from_above.wait_recv()
        finish(held(z) + below[z].astype(f32) + above[z].astype(f32))

    def relay(o):
        here = out_ref.at[o * 2 + y]
        arrived = gather_recv.at[o * 2 + y]
        return (
            remote(here, here, up_send.at[o], arrived, lat + 2, tok),
            remote(here, here, down_send.at[o], arrived, lat - 2, tok),
            remote(here, here, turn_send.at[o], arrived, beside, tok),
        )

    up, down, turn = relay(z)
    pl.when(z < 3)(up.start)
    pl.when(z > 0)(down.start)
    turn.start()
    for s in range(1, 4):
        @pl.when(z - s >= 0)
        def _():
            up, down, turn = relay(z - s)
            turn.wait_recv()
            pl.when(z < 3)(up.start)
            turn.start()

        @pl.when(z + s <= 3)
        def _():
            up, down, turn = relay(z + s)
            turn.wait_recv()
            pl.when(z > 0)(down.start)
            turn.start()

    for o in range(4):
        there = out_ref.at[o * 2 + oy]
        remote(there, there, turn_send.at[o], gather_recv.at[o * 2 + oy], beside, tok).wait_recv()
    for o in range(4):
        up, down, turn = relay(o)
        pl.when(jnp.logical_and(o <= z, z < 3))(up.wait_send)
        pl.when(jnp.logical_and(o >= z, z > 0))(down.wait_send)
        turn.wait_send()
    for swap in swaps:
        swap.wait_send()
    for d, up, down in lines:
        up.wait_send()


def errors_of(w, codes, bias, resid_rows):
    total, tokens = w.shape[1], codes.shape[1]
    rows = total // 8
    return call(
        errors_kernel,
        jax.ShapeDtypeStruct((8, rows, tokens), bf16),
        (w, codes, bias, resid_rows),
        [VMEM((8, w.shape[0], rows), bf16), VMEM((8, rows, tokens), bf16), DMA((8,))]
        + [VMEM((4, rows, tokens), bf16)] * 4 + [DMA((4,))] * 8 + [DMA((8,))],
        4,
        "recon_errors",
        (0,),
    ).reshape(total, tokens)


def small_sum(x):
    pair = x + lax.ppermute(x, "lat", [(n, n + 1 - 2 * (n % 2)) for n in range(8)])
    return pair, [
        lax.ppermute(pair, "lat", [(n, (n + s) % 8) for n in range(8)]) for s in (2, 4, 6)
    ]


def active_rows(ids, base, rows):
    word = 32 if rows % 32 == 0 else rows
    local = ids - base
    which = local // word
    place = local - which * word
    bit = lax.shift_left(jnp.int32(1), place)
    words = lax.iota(jnp.int32, rows // word)
    held = jnp.where(which[None, :, :] == words[:, None, None], bit[None, :, :], 0)
    held = jnp.sum(held, axis=1)
    shifts = lax.iota(jnp.int32, word)
    flags = lax.shift_right_logical(held[:, None, :], jnp.broadcast_to(shifts[None, :, None], (rows // word, word, held.shape[1]))) & 1
    return flags.reshape(rows, held.shape[1]).astype(f32)


def on_device(kernels, resid, active_ids, w_enc, w_dec, b_enc, b_dec):
    block_rows = w_enc.shape[0]
    width = w_enc.shape[1]
    lat_pos = lax.axis_index("lat")
    tok_pos = lax.axis_index("tok")
    tok_count = lax.axis_size("tok")
    lat_count = lax.axis_size("lat")
    rows = block_rows // tok_count
    feats = width // lat_count

    if kernels:
        resid_mine, bias_mine, ids_all = spread(resid, b_dec, active_ids)
    else:
        ids_all = lax.all_gather(active_ids, "tok", axis=0, tiled=True).T
        bias_full = lax.all_gather(b_dec, "lat", axis=0, tiled=True)
        resid_full = lax.all_gather(resid, "lat", axis=0, tiled=True)
        resid_mine = lax.all_to_all(resid_full, "tok", split_axis=0, concat_axis=1, tiled=True)
        bias_mine = lax.dynamic_slice_in_dim(bias_full, tok_pos * width, width, 0).astype(f32)
    centred = (resid_mine.astype(f32) - bias_mine[:, None]).astype(bf16)

    active = active_rows(ids_all, lat_pos * block_rows + tok_pos * rows, rows)
    b_rows = lax.dynamic_slice_in_dim(b_enc, tok_pos * rows, rows, 0)

    if kernels:
        codes = masked_sum(w_enc, centred, b_rows[:, None], active, 2)
    else:
        pre_part = jnp.dot(w_enc, centred, preferred_element_type=f32)
        pre = lax.psum_scatter(pre_part, "tok", scatter_dimension=0, tiled=True)
        codes_rows = ((pre + b_rows[:, None]) * active).astype(bf16)
        codes = lax.all_gather(codes_rows, "tok", axis=0, tiled=True)

    r_rows = lax.dynamic_slice_in_dim(resid_mine, lat_pos * feats, feats, 0)
    bd_rows = lax.dynamic_slice_in_dim(bias_mine, lat_pos * feats, feats, 0)
    bd_rows = bd_rows[:, None]
    if kernels:
        errors = errors_of(w_dec, codes, bd_rows, r_rows)
    else:
        recon_part = lax.dot_general(
            w_dec, codes, (((0,), (0,)), ((), ())), preferred_element_type=f32
        )
        recon = lax.psum_scatter(recon_part, "lat", scatter_dimension=0, tiled=True)
        error_rows = (recon + bd_rows - r_rows.astype(f32)).astype(bf16)
        errors = lax.all_gather(error_rows, "lat", axis=0, tiled=True)

    if kernels:
        grad_pre = masked_sum(w_dec, errors, jnp.zeros((rows, 1), f32), active, 3)
    else:
        gc_part = jnp.dot(w_dec, errors, preferred_element_type=f32)
        gc = lax.psum_scatter(gc_part, "tok", scatter_dimension=0, tiled=True)
        gp_rows = (gc * active).astype(bf16)
        grad_pre = lax.all_gather(gp_rows, "tok", axis=0, tiled=True)

    grad_b_enc = jnp.sum(grad_pre.astype(f32), axis=1)
    high = grad_b_enc.astype(bf16)
    rest = grad_b_enc - high.astype(f32)
    mid = rest.astype(bf16)
    low = (rest - mid.astype(f32)).astype(bf16)
    parts = jnp.stack([high, mid, low])
    back = jnp.sum(jnp.dot(parts, w_enc, preferred_element_type=f32), axis=0)
    if kernels:
        back, others = small_sum(back)
        codes, back = lax.optimization_barrier((codes, back))
        back = back + (others[0] + others[1] + others[2])
    else:
        back = lax.psum(back, "lat")
    grad_w_dec = lax.dot_general(
        codes, errors, (((1,), (1,)), ((), ())), preferred_element_type=f32
    ).astype(bf16)
    error_total = jnp.sum(errors.astype(f32), axis=1)
    grad_w_enc = lax.dot_general(
        grad_pre, centred, (((1,), (1,)), ((), ())), preferred_element_type=f32
    ).astype(bf16)
    return (grad_w_enc, grad_w_dec, grad_b_enc, error_total - back)


def solution(mesh):
    kernels = mesh.shape["lat"] == 8 and mesh.shape["tok"] == 4
    return jax.shard_map(
        functools.partial(on_device, kernels),
        mesh=mesh,
        in_specs=(
            P("lat", "tok"),
            P("tok", None),
            P("lat", "tok"),
            P("lat", "tok"),
            P("lat"),
            P("lat"),
        ),
        out_specs=(P("lat", "tok"), P("lat", "tok"), P("lat"), P("tok")),
        check_vma=False,
    )
```
